32 devices in a mesh: dp: 8 (over z, x), ctx: 4 (over y, core).
Axes of the slice: x: 2, y: 2, z: 4, core: 2. Of those that a mesh axis runs over, the one named last changes fastest.
Arguments:
- tokens: bfloat16 [64, 512, 960], P('dp', 'ctx'), may hold values from -6 to 6
- lengths: int32 [64], P('dp'), may hold values from 256 to 512, as said below
- gain_attn: bfloat16 [960], P('dp'), may hold values from 0.5 to 1.5
- w_query: bfloat16 [960, 960], P('dp', 'ctx'), may hold values from -0.1875 to 0.1875
- w_key: bfloat16 [960, 320], P('dp', 'ctx'), may hold values from -0.1875 to 0.1875
- w_value: bfloat16 [960, 320], P('dp', 'ctx'), may hold values from -0.1875 to 0.1875
- w_out: bfloat16 [960, 960], P('dp', 'ctx'), may hold values from -1.5 to 1.5
- gain_ffn: bfloat16 [960], P('dp'), may hold values from 0.5 to 1.5
- w_gate: bfloat16 [960, 2560], P('dp', 'ctx'), may hold values from -0.1875 to 0.1875
- w_up: bfloat16 [960, 2560], P('dp', 'ctx'), may hold values from -0.1875 to 0.1875
- w_down: bfloat16 [2560, 960], P('dp', 'ctx'), may hold values from -0.125 to 0.125
- grad_out: bfloat16 [64, 512, 960], P('dp', 'ctx'), may hold values from -6 to 6
Outputs:
- output: bfloat16 [64, 512, 960], P('dp', 'ctx')
- grad_tokens: bfloat16 [64, 512, 960], P('dp', 'ctx')
- grad_gain_attn: float32 [960], P('dp')
- grad_w_query: float32 [960, 960], P('dp', 'ctx')
- grad_w_key: float32 [960, 320], P('dp', 'ctx')
- grad_w_value: float32 [960, 320], P('dp', 'ctx')
- grad_w_out: float32 [960, 960], P('dp', 'ctx')
- grad_gain_ffn: float32 [960], P('dp')
- grad_w_gate: float32 [960, 2560], P('dp', 'ctx')
- grad_w_up: float32 [960, 2560], P('dp', 'ctx')
- grad_w_down: float32 [2560, 960], P('dp', 'ctx')
The draws below stay inside these ranges and needn't reach their ends.
Inputs may be any that keep to these rules, and one draw needn't show every extreme that they name: `lengths`: in every aligned group of 8 sequences one is 512 long and one is 256 long.
All inputs are finite; a program needn't handle non-finite values.
Results may differ from the reference program's by a relative error of at most 0.015.
Values may be sent and summed in bfloat16 or wider, within the bound.
A program may use at most 192 MiB of HBM per device.

```python
import math
import jax
import jax.numpy as jnp
from jax import lax

D = 960
HEADS = 15
KV_HEADS = 5
HEAD_DIM = 64
FF = 2560
LEN = 512
SEQ_DEV = 8
SEQS = 64
QW = 960
KVW = 320


def shuffled(key_item):
    return jax.random.permutation(key_item, SEQ_DEV)


def draw_lengths(key, part):
    key = jax.random.fold_in(key, 7)
    first_key, second_key = jax.random.split(key)
    group_count = SEQS // SEQ_DEV
    sampled = jax.random.randint(first_key, (group_count, SEQ_DEV), LEN // 2, LEN + 1, dtype=jnp.int32)
    ranking = jax.vmap(shuffled)(jax.random.split(second_key, group_count))
    chosen = jnp.where(ranking == 0, LEN, jnp.where(ranking == 1, LEN // 2, sampled))
    return chosen.reshape(SEQS).astype(jnp.int32)


def levels(key, extent, cuts, least, largest):
    gain = 1.0
    for dim, parts in cuts:
        draws = jax.random.uniform(jax.random.fold_in(jax.random.fold_in(key, 6), dim), (parts,), jnp.float32, least / len(cuts), largest / len(cuts))
        gain = gain * jnp.repeat(jnp.exp(draws), extent[dim] // parts).reshape((-1,) + (1,) * (len(extent) - 1 - dim))
    return gain


def centred(stream_key, shape, scale, bound, cuts=(), held_as=jnp.bfloat16):
    entries = scale * jax.random.normal(stream_key, shape, jnp.float32)
    if cuts:
        entries = entries * levels(stream_key, shape, cuts, -0.22, 0.18)
    return jnp.clip(entries, -bound, bound).astype(held_as)


def setup_inputs(seed: int = 0) -> dict:
    splits = jax.random.split(jax.random.key(seed), 13)
    return {
        "tokens": centred(splits[0], (SEQS, LEN, D), 1.0, 6.0, ((0, 8), (1, 4))),
        "lengths": draw_lengths(jax.random.fold_in(splits[12], 71), 0),
        "gain_attn": jnp.clip(1.0 + 0.1 * jax.random.normal(splits[2], (D,), jnp.float32), 0.5, 1.5).astype(jnp.bfloat16),
        "w_query": centred(splits[3], (D, QW), D ** -0.5, 0.1875, ((0, 8), (1, 4))),
        "w_key": centred(splits[4], (D, KVW), D ** -0.5, 0.1875, ((0, 8), (1, 4))),
        "w_value": centred(splits[5], (D, KVW), D ** -0.5, 0.1875, ((0, 8), (1, 4))),
        "w_out": centred(splits[6], (QW, D), (QW // 64) ** -0.5, 1.5, ((0, 8), (1, 4))),
        "gain_ffn": jnp.clip(1.0 + 0.1 * jax.random.normal(splits[7], (D,), jnp.float32), 0.5, 1.5).astype(jnp.bfloat16),
        "w_gate": centred(splits[8], (D, FF), D ** -0.5, 0.1875, ((0, 8), (1, 4))),
        "w_up": centred(splits[9], (D, FF), D ** -0.5, 0.1875, ((0, 8), (1, 4))),
        "w_down": centred(splits[10], (FF, D), FF ** -0.5, 0.125, ((0, 8), (1, 4))),
        "grad_out": centred(splits[11], (SEQS, LEN, D), 1.0, 6.0, ((0, 8), (1, 4))),
    }


@jax.custom_vjp
def low(v):
    return lax.optimization_barrier(v.astype(jnp.bfloat16)).astype(jnp.float32)

@jax.custom_vjp
def low_back(v):
    return v

def low_keep(v):
    return (low(v), None)

def low_pass(kept, grad):
    return (grad,)

def back_keep(v):
    return (v, None)

def back_low(kept, grad):
    return (low(grad),)
low.defvjp(low_keep, low_pass)
low_back.defvjp(back_keep, back_low)
EPS = 1e-05
THETA = 100000.0
HIGH = lax.Precision.HIGHEST

def matmul(former, latter):
    return jnp.dot(former, latter, precision=HIGH, preferred_element_type=jnp.float32)

def rms_scale(values, scaling):
    return values * lax.rsqrt(lax.optimization_barrier(jnp.mean(values * values, axis=-1, keepdims=True)) + EPS) * scaling

def rotate(values, cosine, sine_part):
    half_dim = values.shape[-1] // 2
    lower_half = values[..., :half_dim]
    upper_half = values[..., half_dim:]
    return jnp.concatenate([lower_half * cosine - upper_half * sine_part, upper_half * cosine + lower_half * sine_part], axis=-1)

def block_forward(inputs, valid_len, cosine, sine_part, gain_one, w_query, w_key, w_value, w_out, gain_two, w_gate, w_up, w_down):
    seq_count, length, width = inputs.shape
    per_kv = HEADS // KV_HEADS
    normed_attn = low(rms_scale(inputs, gain_one)).reshape(seq_count * length, width)
    queries = low_back(matmul(normed_attn, w_query)).reshape(seq_count, length, KV_HEADS, per_kv, HEAD_DIM)
    queries = low(rotate(queries, cosine[:, None, None, :], sine_part[:, None, None, :]))
    keys_all = low_back(matmul(normed_attn, w_key)).reshape(seq_count, length, KV_HEADS, HEAD_DIM)
    keys_all = low(rotate(keys_all, cosine[:, None, :], sine_part[:, None, :]))
    values_all = low(low_back(matmul(normed_attn, w_value))).reshape(seq_count, length, KV_HEADS, HEAD_DIM)
    scores = low_back(HEAD_DIM ** (-0.5) * jnp.einsum('sqhgd,skhd->shgqk', queries, keys_all, precision=HIGH))
    positions = jnp.arange(length, dtype=jnp.int32)
    causal = positions[None, :] <= positions[:, None]
    allowed = causal[None, None, None] & (positions[None, None, None, None, :] < valid_len[:, None, None, None, None])
    masked = jnp.where(allowed, scores, -1e+30)
    peak = lax.optimization_barrier(jnp.max(masked, axis=-1, keepdims=True))
    raised = jnp.exp(masked - peak)
    shares = low(raised / lax.optimization_barrier(jnp.sum(raised, axis=-1, keepdims=True)))
    attended = jnp.einsum('shgqk,skhd->sqhgd', shares, values_all, precision=HIGH)
    attended = low(low_back(attended)).reshape(seq_count * length, HEADS * HEAD_DIM)
    hidden = inputs + low_back(matmul(attended, w_out)).reshape(seq_count, length, width)
    normed_ffn = low(rms_scale(hidden, gain_two)).reshape(seq_count * length, width)
    gating = low_back(matmul(normed_ffn, w_gate))
    up_proj = low_back(matmul(normed_ffn, w_up))
    inner = low(gating * jax.nn.sigmoid(gating) * up_proj)
    return hidden + low_back(matmul(inner, w_down)).reshape(seq_count, length, width)

def reference(tokens, lengths, gain_attn, w_query, w_key, w_value, w_out, gain_ffn, w_gate, w_up, w_down, grad_out):
    params = tuple((weight_arg.astype(jnp.float32) for weight_arg in (gain_attn, w_query, w_key, w_value, w_out, gain_ffn, w_gate, w_up, w_down)))
    half_dim = HEAD_DIM // 2
    inverse = THETA ** (-(jnp.arange(half_dim, dtype=jnp.float32) * 2.0 / HEAD_DIM))
    angles = jnp.arange(LEN, dtype=jnp.int32).astype(jnp.float32)[:, None] * inverse[None, :]
    cosine = jnp.cos(angles)
    sine_part = jnp.sin(angles)
    group_size = math.gcd(SEQS, max(1, 4096 // LEN))
    steps_count = SEQS // group_size

    def shaped(array):
        return array.reshape((steps_count, group_size) + array.shape[1:])

    def accumulate(carry, batch_in):
        seq_in, valid_len, seq_grad = batch_in

        def forward_fn(inputs, *weights):
            return block_forward(inputs, valid_len, cosine, sine_part, *weights)
        result, pull = jax.vjp(forward_fn, seq_in.astype(jnp.float32), *params)
        grads = pull(seq_grad.astype(jnp.float32))
        carry = tuple((before + after for before, after in zip(carry, grads[1:])))
        return (carry, (result.astype(jnp.bfloat16), grads[0].astype(jnp.bfloat16)))
    zero_grads = tuple((jnp.zeros_like(param) for param in params))
    totals, (results, input_grads) = lax.scan(accumulate, zero_grads, (shaped(tokens), shaped(lengths), shaped(grad_out)))
    results = results.reshape(SEQS, LEN, D)
    input_grads = input_grads.reshape(SEQS, LEN, D)
    return (results, input_grads, totals[0], totals[1], totals[2], totals[3], totals[4], totals[5], totals[6], totals[7], totals[8])
```

```python
from functools import partial

import jax
import jax.numpy as jnp
from jax import lax
from jax.experimental import pallas as pl
from jax.experimental.pallas import tpu as pltpu
from jax.sharding import PartitionSpec as P

HEADS = 15
KV_HEADS = 5
HEAD_DIM = 64
PAIR = 2
PIECES = 4
MESH = pl.DeviceIdType.MESH

EPS = 1e-05
THETA = 100000.0


def product(former, latter):
    return jnp.dot(former, latter, preferred_element_type=jnp.float32)


def against(former, latter):
    return lax.dot_general(
        former, latter, (((1,), (1,)), ((), ())), preferred_element_type=jnp.float32
    )


def outer_sum(former, latter):
    return lax.dot_general(
        former, latter, (((0,), (0,)), ((), ())), preferred_element_type=jnp.float32
    )


def rms_scale(values, scaling):
    return values * lax.rsqrt(jnp.mean(values * values, axis=-1, keepdims=True) + EPS) * scaling


def rotate(values, cosine, sine_part):
    half_dim = values.shape[-1] // 2
    lower_half = values[..., :half_dim]
    upper_half = values[..., half_dim:]
    return jnp.concatenate(
        [
            lower_half * cosine - upper_half * sine_part,
            upper_half * cosine + lower_half * sine_part,
        ],
        axis=-1,
    )


def silu_gate(gating, up_proj):
    return gating * jax.nn.sigmoid(gating) * up_proj


def place():
    dp, ctx = lax.axis_index("dp"), lax.axis_index("ctx")
    return dp // PAIR, dp % PAIR, ctx // PAIR, ctx % PAIR


def device(z, x, y, c):
    return (z * PAIR + x, y * PAIR + c)


def remote(source, target, send_sem, recv_sem, where):
    return pltpu.make_async_remote_copy(
        src_ref=source,
        dst_ref=target,
        send_sem=send_sem,
        recv_sem=recv_sem,
        device_id=where,
        device_id_type=MESH,
    )


def greet(z, x, y, c, depth):
    barrier = pltpu.get_barrier_semaphore()
    for where in (device(z, 1 - x, y, c), device(z, x, 1 - y, c), device(z, x, y, 1 - c)):
        pl.semaphore_signal(barrier, inc=1, device_id=where, device_id_type=MESH)

    @pl.when(z > 0)
    def _():
        pl.semaphore_signal(barrier, inc=1, device_id=device(z - 1, x, y, c), device_id_type=MESH)

    @pl.when(z < depth - 1)
    def _():
        pl.semaphore_signal(barrier, inc=1, device_id=device(z + 1, x, y, c), device_id_type=MESH)

    pl.semaphore_wait(barrier, 3 + jnp.minimum(z, 1) + jnp.minimum(depth - 1 - z, 1))


def gather_kernel(*refs):
    shards, fulls = refs[:PIECES], refs[PIECES : 2 * PIECES]
    local, z_send, z_recv, f_send, f_recv, s_send, s_recv, c_send, c_recv = refs[2 * PIECES :]
    depth = fulls[0].shape[2]
    z, x, y, c = place()
    greet(z, x, y, c, depth)

    def along_z(p, way, owner):
        shard = fulls[p].at[y, c, owner, x]
        return remote(
            shard,
            shard,
            z_send.at[way, p, owner],
            z_recv.at[way, p, owner],
            device(z + (1 if way == 0 else -1), x, y, c),
        )

    def where_to(p, f_side, s_side):
        if p % 2 == 0:
            return (x if f_side == 0 else 1 - x), (y if s_side == 0 else 1 - y)
        return (x if s_side == 0 else 1 - x), (y if f_side == 0 else 1 - y)

    def unit(p, f_side, s_side, core):
        ux, uy = where_to(p, f_side, s_side)
        return fulls[p].at[uy, core, :, ux]

    def first(p):
        ux, uy = where_to(p, 1, 0)
        mine = unit(p, 0, 0, c)
        return remote(mine, mine, f_send.at[p], f_recv.at[p], device(z, ux, uy, c))

    def second(p, f_side):
        ux, uy = where_to(p, 0, 1)
        held = unit(p, f_side, 0, c)
        return remote(
            held, held, s_send.at[p, f_side], s_recv.at[p, f_side], device(z, ux, uy, c)
        )

    def across(p, f_side, s_side):
        held = unit(p, f_side, s_side, c)
        slot = 2 * s_side + f_side
        return remote(
            held, held, c_send.at[p, slot], c_recv.at[p, slot], device(z, x, y, 1 - c)
        )

    owns = []
    for p in range(PIECES):
        own = pltpu.make_async_copy(shards[p], fulls[p].at[y, c, z, x], local.at[p])
        own.start()
        owns.append(own)
    for p in range(PIECES):
        owns[p].wait()

        @pl.when(z < depth - 1)
        def _():
            along_z(p, 0, z).start()

        @pl.when(z > 0)
        def _():
            along_z(p, 1, z).start()

    def z_stage(p):
        def step(s, carry):
            @pl.when(z - s >= 0)
            def _():
                along_z(p, 0, z - s).wait_recv()

                @pl.when(z < depth - 1)
                def _():
                    along_z(p, 0, z - s).start()

            @pl.when(z + s < depth)
            def _():
                along_z(p, 1, z + s).wait_recv()

                @pl.when(z > 0)
                def _():
                    along_z(p, 1, z + s).start()

            return carry

        lax.fori_loop(1, depth, step, 0)
        first(p).start()
        second(p, 0).start()
        across(p, 0, 0).start()

    def f_stage(p):
        first(p).wait_recv()
        second(p, 1).start()
        across(p, 1, 0).start()

    def s_stage(p):
        for f_side in range(2):
            second(p, f_side).wait_recv()
            across(p, f_side, 1).start()

    z_stage(0)
    z_stage(1)
    z_stage(2)
    f_stage(0)
    f_stage(1)
    z_stage(3)
    f_stage(2)
    f_stage(3)
    for p in range(PIECES):
        s_stage(p)
    for p in range(PIECES):
        for slot in range(4):
            across(p, slot % 2, slot // 2).wait()
        first(p).wait_send()
        second(p, 0).wait_send()
        second(p, 1).wait_send()

        def drain(owner, carry):
            @pl.when((owner <= z) & (z < depth - 1))
            def _():
                along_z(p, 0, owner).wait_send()

            @pl.when((owner >= z) & (z > 0))
            def _():
                along_z(p, 1, owner).wait_send()

            return carry

        lax.fori_loop(0, depth, drain, 0)


def gather(shards):
    dp, ctx = lax.axis_size("dp"), lax.axis_size("ctx")
    lead = (ctx // PAIR, PAIR, dp // PAIR, PAIR)
    dma = pltpu.SemaphoreType.DMA
    return pl.pallas_call(
        gather_kernel,
        out_shape=[jax.ShapeDtypeStruct(lead + shard.shape, shard.dtype) for shard in shards],
        in_specs=[pl.BlockSpec(memory_space=pl.ANY)] * PIECES,
        out_specs=[pl.BlockSpec(memory_space=pl.ANY)] * PIECES,
        scratch_shapes=[
            dma((PIECES,)),
            dma((2, PIECES, lead[2])),
            dma((2, PIECES, lead[2])),
            dma((PIECES,)),
            dma((PIECES,)),
            dma((PIECES, 2)),
            dma((PIECES, 2)),
            dma((PIECES, 4)),
            dma((PIECES, 4)),
        ],
        compiler_params=pltpu.CompilerParams(collective_id=0, has_side_effects=True),
        name="weight_gather",
    )(*shards)


def scatter_kernel(*refs):
    grads, sums = refs[:PIECES], refs[PIECES : 2 * PIECES]
    rest = refs[2 * PIECES :]
    locals_, cores, seconds, firsts, lines = (
        rest[i * PIECES : (i + 1) * PIECES] for i in range(5)
    )
    l_sem, z_send, z_recv, f_send, f_recv, s_send, s_recv, c_send, c_recv = rest[5 * PIECES :]
    depth = grads[0].shape[2]
    z, x, y, c = place()

    def sides(p):
        return (x, y) if p % 2 == 0 else (y, x)

    def block(p, f, s, core):
        return grads[p].at[s, core, :, f] if p % 2 == 0 else grads[p].at[f, core, :, s]

    def own(p, f_side, s_side):
        f, s = sides(p)
        f = f if f_side == 0 else 1 - f
        s = s if s_side == 0 else 1 - s
        slot = 2 * s_side + f_side
        return pltpu.make_async_copy(
            block(p, f, s, c), locals_[p].at[slot], l_sem.at[p, slot]
        )

    def across(p, f_side, s_side):
        f, s = sides(p)
        f = f if f_side == 0 else 1 - f
        s = s if s_side == 0 else 1 - s
        slot = 2 * s_side + f_side
        return remote(
            block(p, f, s, 1 - c),
            cores[p].at[slot],
            c_send.at[p, slot],
            c_recv.at[p, slot],
            device(z, x, y, 1 - c),
        )

    def second(p, f_side):
        where = device(z, x, 1 - y, c) if p % 2 == 0 else device(z, 1 - x, y, c)
        return remote(
            cores[p].at[2 + f_side],
            seconds[p].at[f_side],
            s_send.at[p, f_side],
            s_recv.at[p, f_side],
            where,
        )

    def first(p):
        where = device(z, 1 - x, y, c) if p % 2 == 0 else device(z, x, 1 - y, c)
        return remote(seconds[p].at[1], firsts[p], f_send.at[p], f_recv.at[p], where)

    def along_z(p, way, goal, source):
        return remote(
            source,
            lines[p].at[way, goal],
            z_send.at[way, p, goal],
            z_recv.at[way, p, goal],
            device(z + (1 if way == 0 else -1), x, y, c),
        )

    def add(target, source):
        def step(i, carry):
            total = target[i].astype(jnp.float32) + source[i].astype(jnp.float32)
            target[i] = total.astype(jnp.bfloat16)
            return carry

        lax.fori_loop(0, depth, step, 0)

    for p in range(PIECES):
        for slot in (3, 2, 1, 0):
            own(p, slot % 2, slot // 2).start()
    greet(z, x, y, c, depth)
    for p in range(PIECES):
        for slot in (3, 2, 1, 0):
            across(p, slot % 2, slot // 2).start()

    def core_sum(p, slot):
        own(p, slot % 2, slot // 2).wait()
        across(p, slot % 2, slot // 2).wait_recv()
        add(cores[p].at[slot], locals_[p].at[slot])

    def s_stage(p):
        for f_side in (1, 0):
            core_sum(p, 2 + f_side)
            second(p, f_side).start()

    def f_stage(p):
        for f_side in (1, 0):
            core_sum(p, f_side)
            second(p, f_side).wait_recv()
            add(seconds[p].at[f_side], cores[p].at[f_side])
            if f_side == 1:
                first(p).start()

    def pass_on(p, way, goal, has_before):
        @pl.when(has_before)
        def _():
            along_z(p, way, goal, lines[p].at[way, goal]).wait_recv()
            total = lines[p][way, goal].astype(jnp.float32) + firsts[p][goal].astype(jnp.float32)
            lines[p][way, goal] = total.astype(jnp.bfloat16)
            along_z(p, way, goal, lines[p].at[way, goal]).start()

        @pl.when(jnp.logical_not(has_before))
        def _():
            along_z(p, way, goal, firsts[p].at[goal]).start()

    def z_stage(p):
        first(p).wait_recv()
        add(firsts[p], seconds[p].at[0])

        def step(s, carry):
            @pl.when(z < depth - s)
            def _():
                pass_on(p, 0, depth - s, z > 0)

            @pl.when(z > s - 1)
            def _():
                pass_on(p, 1, s - 1, z < depth - 1)

            return carry

        lax.fori_loop(1, depth, step, 0)

    def finish(p):
        sums[p][...] = firsts[p][z].astype(jnp.float32)

        @pl.when(z > 0)
        def _():
            along_z(p, 0, z, lines[p].at[0, z]).wait_recv()
            sums[p][...] += lines[p][0, z].astype(jnp.float32)

        @pl.when(z < depth - 1)
        def _():
            along_z(p, 1, z, lines[p].at[1, z]).wait_recv()
            sums[p][...] += lines[p][1, z].astype(jnp.float32)

    for p in range(PIECES):
        s_stage(p)
    for p in range(PIECES):
        f_stage(p)
        if p > 0:
            z_stage(p - 1)
    z_stage(PIECES - 1)
    for p in range(PIECES):
        finish(p)
    for p in range(PIECES):
        for slot in range(4):
            across(p, slot % 2, slot // 2).wait_send()
        second(p, 0).wait_send()
        second(p, 1).wait_send()
        first(p).wait_send()

        def drain(goal, carry):
            @pl.when(goal > z)
            def _():
                along_z(p, 0, goal, firsts[p].at[goal]).wait_send()

            @pl.when(goal < z)
            def _():
                along_z(p, 1, goal, firsts[p].at[goal]).wait_send()

            return carry

        lax.fori_loop(0, depth, drain, 0)


def scatter(grads):
    depth = grads[0].shape[2]
    dma = pltpu.SemaphoreType.DMA
    shapes = [grad.shape[4:] for grad in grads]

    def slots(lead):
        return [pltpu.VMEM(lead + (depth,) + shape, jnp.bfloat16) for shape in shapes]

    return pl.pallas_call(
        scatter_kernel,
        out_shape=[jax.ShapeDtypeStruct(shape, jnp.float32) for shape in shapes],
        in_specs=[pl.BlockSpec(memory_space=pl.ANY)] * PIECES,
        out_specs=[pl.BlockSpec(memory_space=pltpu.VMEM)] * PIECES,
        scratch_shapes=slots((4,))
        + slots((4,))
        + slots((2,))
        + slots(())
        + slots((2,))
        + [
            dma((PIECES, 4)),
            dma((2, PIECES, depth)),
            dma((2, PIECES, depth)),
            dma((PIECES,)),
            dma((PIECES,)),
            dma((PIECES, 2)),
            dma((PIECES, 2)),
            dma((PIECES, 4)),
            dma((PIECES, 4)),
        ],
        compiler_params=pltpu.CompilerParams(
            collective_id=1, has_side_effects=True, vmem_limit_bytes=58 * 1024 * 1024
        ),
        name="grad_scatter",
    )(*grads)


EXTRA = 8


def fetch(gain_attn, w_query, w_key, w_value, w_out, gain_ffn, w_gate, w_up, w_down):
    rows = w_query.shape[0]
    mixed = jnp.concatenate([w_query, w_key, w_value, w_out], axis=1)
    gains = jnp.pad(
        jnp.stack([gain_attn, gain_ffn]), ((0, EXTRA - 2), (0, mixed.shape[1] - rows))
    )
    full_mixed, full_gate, full_up, full_down = gather(
        [jnp.concatenate([mixed, gains], axis=0), w_gate, w_up, w_down]
    )
    dp, ctx = lax.axis_size("dp"), lax.axis_size("ctx")

    def whole(array):
        array = array.reshape((ctx, dp) + array.shape[4:])
        return jnp.transpose(array, (1, 2, 0, 3)).reshape(dp * array.shape[2], -1)

    full_mixed = full_mixed.reshape((ctx, dp) + full_mixed.shape[4:])
    one = full_mixed[0, :, rows, :rows].reshape(-1)
    two = full_mixed[0, :, rows + 1, :rows].reshape(-1)
    full_mixed = full_mixed[:, :, :rows]
    parts = []
    low = 0
    for weight in (w_query, w_key, w_value, w_out):
        wide = weight.shape[1]
        part = jnp.transpose(full_mixed[..., low : low + wide], (1, 2, 0, 3))
        parts.append(part.reshape(dp * rows, ctx * wide))
        low += wide
    return (*parts, whole(full_gate), whole(full_up), whole(full_down), one, two)


def settle(
    grad_one, grad_query, grad_key, grad_value, grad_out, grad_two, grad_gate, grad_up, grad_down
):
    dp, ctx = lax.axis_size("dp"), lax.axis_size("ctx")
    lead = (ctx // PAIR, PAIR, dp // PAIR, PAIR)

    def blocks(array):
        rows, wide = array.shape[0] // dp, array.shape[1] // ctx
        array = array.astype(jnp.bfloat16).reshape(dp, rows, ctx, wide)
        return jnp.transpose(array, (2, 0, 1, 3))

    mixed = jnp.concatenate(
        [blocks(array) for array in (grad_query, grad_key, grad_value, grad_out)], axis=3
    )
    rows, wide = mixed.shape[2:]
    gains = jnp.stack([grad_one.reshape(dp, rows), grad_two.reshape(dp, rows)], axis=1)
    gains = jnp.pad(gains.astype(jnp.bfloat16), ((0, 0), (0, EXTRA - 2), (0, wide - rows)))
    gains = jnp.broadcast_to(gains[None], (ctx,) + gains.shape)
    mixed = jnp.concatenate([mixed, gains], axis=2)
    pieces = [mixed, blocks(grad_gate), blocks(grad_up), blocks(grad_down)]
    own_mixed, own_gate, own_up, own_down = scatter(
        [piece.reshape(lead + piece.shape[2:]) for piece in pieces]
    )
    cuts = []
    low = 0
    for grad in (grad_query, grad_key, grad_value, grad_out):
        high = low + grad.shape[1] // ctx
        cuts.append(own_mixed[:rows, low:high])
        low = high
    return (
        own_mixed[rows, :rows],
        *cuts,
        own_mixed[rows + 1, :rows],
        own_gate,
        own_up,
        own_down,
    )


def masked_scores(queries, key_block, allowed, factor):
    scores = (
        jnp.einsum("mcgd,mld->mgcl", queries, key_block, preferred_element_type=jnp.float32)
        * factor
    )
    return jnp.where(allowed, scores, -1e30)


def attend(operands, allowed, factor):
    queries, key_block, value_block = operands
    scores = masked_scores(queries, key_block, allowed, factor)
    peak = jnp.max(scores, axis=-1, keepdims=True)
    raised = jnp.exp(scores - peak)
    summed = jnp.sum(raised, axis=-1, keepdims=True)
    shares = (raised / summed).astype(jnp.bfloat16)
    blended = jnp.einsum("mgcl,mld->mcgd", shares, value_block, preferred_element_type=jnp.float32)
    return (blended.astype(jnp.bfloat16), peak + jnp.log(summed))


def attend_back(operands, allowed, factor):
    queries, key_block, value_block, upstream, logsum = operands
    scores = masked_scores(queries, key_block, allowed, factor)
    shares = jnp.exp(scores - logsum)
    d_values = jnp.einsum(
        "mgcl,mcgd->mld", shares.astype(jnp.bfloat16), upstream, preferred_element_type=jnp.float32
    )
    d_shares = jnp.einsum(
        "mcgd,mld->mgcl", upstream, value_block, preferred_element_type=jnp.float32
    )
    row_dot = jnp.sum(d_shares * shares, axis=-1, keepdims=True)
    d_scores = (shares * (d_shares - row_dot)).astype(jnp.bfloat16)
    d_queries = (
        jnp.einsum("mgcl,mld->mcgd", d_scores, key_block, preferred_element_type=jnp.float32)
        * factor
    )
    d_keys = (
        jnp.einsum("mgcl,mcgd->mld", d_scores, queries, preferred_element_type=jnp.float32) * factor
    )
    return (d_queries, d_keys, d_values)


def on_device(
    tokens,
    lengths,
    gain_attn,
    w_query,
    w_key,
    w_value,
    w_out,
    gain_ffn,
    w_gate,
    w_up,
    w_down,
    grad_out,
):
    seq_count, span_len, width = tokens.shape
    groups = lax.axis_size("ctx")
    length = span_len * groups
    ctx_rank = lax.axis_index("ctx")
    batch_size = seq_count
    per_kv = HEADS // KV_HEADS
    query_width = HEADS * HEAD_DIM
    key_width = KV_HEADS * HEAD_DIM
    factor = HEAD_DIM ** (-0.5)
    half_dim = HEAD_DIM // 2
    inverse = THETA ** (-(jnp.arange(half_dim, dtype=jnp.float32) * 2.0 / HEAD_DIM))
    query_pos = ctx_rank * span_len + jnp.arange(span_len, dtype=jnp.int32)
    angles = query_pos.astype(jnp.float32)[:, None] * inverse[None, :]
    cosine = jnp.cos(angles)
    sine_part = jnp.sin(angles)
    cos_query = cosine[:, None, None, :]
    sin_query = sine_part[:, None, None, :]
    cos_key = cosine[:, None, :]
    sin_key = sine_part[:, None, :]
    key_pos = jnp.arange(length, dtype=jnp.int32)
    causal = key_pos[None, :] <= query_pos[:, None]
    rows = batch_size * span_len
    shards = (gain_attn, w_query, w_key, w_value, w_out, gain_ffn, w_gate, w_up, w_down)
    forward_weights = fetch(*shards)
    (
        full_query,
        full_key,
        full_value,
        full_out,
        full_gate,
        full_up,
        full_down,
        full_one,
        full_two,
    ) = forward_weights
    gain_one = full_one.astype(jnp.float32)
    gain_two = full_two.astype(jnp.float32)
    inputs = tokens.astype(jnp.float32).reshape(rows, width)
    valid_len = lengths
    allowed = causal[None, None] & (
        key_pos[None, None, None, :] < valid_len[:, None, None, None]
    )
    normed_attn = rms_scale(inputs, gain_one).astype(jnp.bfloat16)
    queries = product(normed_attn, full_query).reshape(
        batch_size, span_len, KV_HEADS, per_kv, HEAD_DIM
    )
    queries = rotate(queries, cos_query, sin_query).astype(jnp.bfloat16)
    key_own = product(normed_attn, full_key).reshape(batch_size, span_len, KV_HEADS, HEAD_DIM)
    key_own = (
        rotate(key_own, cos_key, sin_key)
        .astype(jnp.bfloat16)
        .reshape(batch_size, span_len, key_width)
    )
    value_own = (
        product(normed_attn, full_value)
        .astype(jnp.bfloat16)
        .reshape(batch_size, span_len, key_width)
    )
    key_all, value_all = (
        lax.all_gather(key_own, "ctx", axis=1, tiled=True),
        lax.all_gather(value_own, "ctx", axis=1, tiled=True),
    )
    head_query = jnp.moveaxis(queries, 2, 0)
    head_key = jnp.moveaxis(key_all.reshape(batch_size, length, KV_HEADS, HEAD_DIM), 2, 0)
    head_value = jnp.moveaxis(value_all.reshape(batch_size, length, KV_HEADS, HEAD_DIM), 2, 0)
    blended, logsum = lax.map(
        partial(attend, allowed=allowed, factor=factor), (head_query, head_key, head_value)
    )
    attended = jnp.moveaxis(blended, 0, 2).reshape(rows, query_width)
    hidden = inputs + product(attended, full_out)
    normed_ffn = rms_scale(hidden, gain_two).astype(jnp.bfloat16)
    gating = product(normed_ffn, full_gate)
    up_proj = product(normed_ffn, full_up)
    inner = silu_gate(gating, up_proj).astype(jnp.bfloat16)
    result = hidden + product(inner, full_down)
    output_all = result.astype(jnp.bfloat16).reshape(batch_size, span_len, width)
    upstream = grad_out.astype(jnp.float32).reshape(rows, width)
    d_down = upstream.astype(jnp.bfloat16)
    grad_down = outer_sum(inner, d_down)
    d_inner = against(d_down, full_down)
    gate_pull = jax.vjp(silu_gate, gating, up_proj)[1]
    d_gating, d_up = gate_pull(d_inner)
    d_gating = d_gating.astype(jnp.bfloat16)
    d_up = d_up.astype(jnp.bfloat16)
    grad_gate = outer_sum(normed_ffn, d_gating)
    grad_up = outer_sum(normed_ffn, d_up)
    d_normed_ffn = against(d_gating, full_gate) + against(d_up, full_up)
    ffn_pull = jax.vjp(rms_scale, hidden, full_two.astype(jnp.float32))[1]
    d_hidden_part, grad_two = ffn_pull(d_normed_ffn)
    d_hidden = upstream + d_hidden_part
    d_attn = d_hidden.astype(jnp.bfloat16)
    grad_out_w = outer_sum(attended, d_attn)
    d_attended = against(d_attn, full_out).astype(jnp.bfloat16)
    head_upstream = jnp.moveaxis(
        d_attended.reshape(batch_size, span_len, KV_HEADS, per_kv, HEAD_DIM), 2, 0
    )
    d_query_h, d_key_h, d_value_h = lax.map(
        partial(attend_back, allowed=allowed, factor=factor),
        (head_query, head_key, head_value, head_upstream, logsum),
    )
    d_key_full = jnp.moveaxis(d_key_h, 0, 2).reshape(batch_size, length, key_width)
    d_value_full = jnp.moveaxis(d_value_h, 0, 2).reshape(batch_size, length, key_width)
    d_key_own, d_value_own = (
        lax.psum_scatter(d_key_full, "ctx", scatter_dimension=1, tiled=True),
        lax.psum_scatter(d_value_full, "ctx", scatter_dimension=1, tiled=True),
    )
    d_query = (
        rotate(jnp.moveaxis(d_query_h, 0, 2), cos_query, -sin_query)
        .astype(jnp.bfloat16)
        .reshape(rows, query_width)
    )
    d_key = (
        rotate(d_key_own.reshape(batch_size, span_len, KV_HEADS, HEAD_DIM), cos_key, -sin_key)
        .astype(jnp.bfloat16)
        .reshape(rows, key_width)
    )
    d_value = d_value_own.astype(jnp.bfloat16).reshape(rows, key_width)
    grad_query = outer_sum(normed_attn, d_query)
    grad_key = outer_sum(normed_attn, d_key)
    grad_value = outer_sum(normed_attn, d_value)
    d_normed_attn = (
        against(d_query, full_query) + against(d_key, full_key) + against(d_value, full_value)
    )
    attn_pull = jax.vjp(rms_scale, inputs, full_one.astype(jnp.float32))[1]
    d_input_part, grad_one = attn_pull(d_normed_attn)
    grads_all = (d_hidden + d_input_part).astype(jnp.bfloat16).reshape(batch_size, span_len, width)
    local_grads = (
        grad_one,
        grad_query,
        grad_key,
        grad_value,
        grad_out_w,
        grad_two,
        grad_gate,
        grad_up,
        grad_down,
    )
    owned = settle(*local_grads)
    return (
        output_all,
        grads_all,
        owned[0],
        owned[1],
        owned[2],
        owned[3],
        owned[4],
        owned[5],
        owned[6],
        owned[7],
        owned[8],
    )


def solution(mesh):
    return jax.shard_map(
        on_device,
        mesh=mesh,
        in_specs=(
            P("dp", "ctx", None),
            P("dp"),
            P("dp"),
            P("dp", "ctx"),
            P("dp", "ctx"),
            P("dp", "ctx"),
            P("dp", "ctx"),
            P("dp"),
            P("dp", "ctx"),
            P("dp", "ctx"),
            P("dp", "ctx"),
            P("dp", "ctx", None),
        ),
        out_specs=(
            P("dp", "ctx", None),
            P("dp", "ctx", None),
            P("dp"),
            P("dp", "ctx"),
            P("dp", "ctx"),
            P("dp", "ctx"),
            P("dp", "ctx"),
            P("dp"),
            P("dp", "ctx"),
            P("dp", "ctx"),
            P("dp", "ctx"),
        ),
        check_vma=False,
    )
```

```python
from functools import partial

import jax
import jax.numpy as jnp
from jax import lax
from jax.experimental import pallas as pl
from jax.experimental.pallas import tpu as pltpu
from jax.sharding import PartitionSpec as P

HEADS = 15
KV_HEADS = 5
HEAD_DIM = 64
PAIR = 2
PIECES = 4
MESH = pl.DeviceIdType.MESH

EPS = 1e-05
THETA = 100000.0


def product(former, latter):
    return jnp.dot(former, latter, preferred_element_type=jnp.float32)


def against(former, latter):
    return lax.dot_general(
        former, latter, (((1,), (1,)), ((), ())), preferred_element_type=jnp.float32
    )


def outer_sum(former, latter):
    return lax.dot_general(
        former, latter, (((0,), (0,)), ((), ())), preferred_element_type=jnp.float32
    )


def rms_scale(values, scaling):
    return values * lax.rsqrt(jnp.mean(values * values, axis=-1, keepdims=True) + EPS) * scaling


def rotate(values, cosine, sine_part):
    half_dim = values.shape[-1] // 2
    lower_half = values[..., :half_dim]
    upper_half = values[..., half_dim:]
    return jnp.concatenate(
        [
            lower_half * cosine - upper_half * sine_part,
            upper_half * cosine + lower_half * sine_part,
        ],
        axis=-1,
    )


def silu_gate(gating, up_proj):
    return gating * jax.nn.sigmoid(gating) * up_proj


def place():
    dp, ctx = lax.axis_index("dp"), lax.axis_index("ctx")
    return dp // PAIR, dp % PAIR, ctx // PAIR, ctx % PAIR


def device(z, x, y, c):
    return (z * PAIR + x, y * PAIR + c)


def remote(source, target, send_sem, recv_sem, where):
    return pltpu.make_async_remote_copy(
        src_ref=source,
        dst_ref=target,
        send_sem=send_sem,
        recv_sem=recv_sem,
        device_id=where,
        device_id_type=MESH,
    )


def greet(z, x, y, c, depth):
    barrier = pltpu.get_barrier_semaphore()
    for where in (device(z, 1 - x, y, c), device(z, x, 1 - y, c), device(z, x, y, 1 - c)):
        pl.semaphore_signal(barrier, inc=1, device_id=where, device_id_type=MESH)

    @pl.when(z > 0)
    def _():
        pl.semaphore_signal(barrier, inc=1, device_id=device(z - 1, x, y, c), device_id_type=MESH)

    @pl.when(z < depth - 1)
    def _():
        pl.semaphore_signal(barrier, inc=1, device_id=device(z + 1, x, y, c), device_id_type=MESH)

    pl.semaphore_wait(barrier, 3 + jnp.minimum(z, 1) + jnp.minimum(depth - 1 - z, 1))


def gather_kernel(*refs):
    shards, fulls = refs[:PIECES], refs[PIECES : 2 * PIECES]
    local, z_send, z_recv, f_send, f_recv, s_send, s_recv, c_send, c_recv = refs[2 * PIECES :]
    depth = fulls[0].shape[2]
    z, x, y, c = place()
    greet(z, x, y, c, depth)

    def along_z(p, way, owner):
        shard = fulls[p].at[y, c, owner, x]
        return remote(
            shard,
            shard,
            z_send.at[way, p, owner],
            z_recv.at[way, p, owner],
            device(z + (1 if way == 0 else -1), x, y, c),
        )

    def where_to(p, f_side, s_side):
        if p % 2 == 0:
            return (x if f_side == 0 else 1 - x), (y if s_side == 0 else 1 - y)
        return (x if s_side == 0 else 1 - x), (y if f_side == 0 else 1 - y)

    def unit(p, f_side, s_side, core):
        ux, uy = where_to(p, f_side, s_side)
        return fulls[p].at[uy, core, :, ux]

    def first(p):
        ux, uy = where_to(p, 1, 0)
        mine = unit(p, 0, 0, c)
        return remote(mine, mine, f_send.at[p], f_recv.at[p], device(z, ux, uy, c))

    def second(p, f_side):
        ux, uy = where_to(p, 0, 1)
        held = unit(p, f_side, 0, c)
        return remote(
            held, held, s_send.at[p, f_side], s_recv.at[p, f_side], device(z, ux, uy, c)
        )

    def across(p, f_side, s_side):
        held = unit(p, f_side, s_side, c)
        slot = 2 * s_side + f_side
        return remote(
            held, held, c_send.at[p, slot], c_recv.at[p, slot], device(z, x, y, 1 - c)
        )

    owns = []
    for p in range(PIECES):
        own = pltpu.make_async_copy(shards[p], fulls[p].at[y, c, z, x], local.at[p])
        own.start()
        owns.append(own)
    for p in range(PIECES):
        owns[p].wait()

        @pl.when(z < depth - 1)
        def _():
            along_z(p, 0, z).start()

        @pl.when(z > 0)
        def _():
            along_z(p, 1, z).start()

    def z_stage(p):
        def step(s, carry):
            @pl.when(z - s >= 0)
            def _():
                along_z(p, 0, z - s).wait_recv()

                @pl.when(z < depth - 1)
                def _():
                    along_z(p, 0, z - s).start()

            @pl.when(z + s < depth)
            def _():
                along_z(p, 1, z + s).wait_recv()

                @pl.when(z > 0)
                def _():
                    along_z(p, 1, z + s).start()

            return carry

        lax.fori_loop(1, depth, step, 0)
        first(p).start()
        second(p, 0).start()
        across(p, 0, 0).start()

    def f_stage(p):
        first(p).wait_recv()
        second(p, 1).start()
        across(p, 1, 0).start()

    def s_stage(p):
        for f_side in range(2):
            second(p, f_side).wait_recv()
            across(p, f_side, 1).start()

    z_stage(0)
    z_stage(1)
    z_stage(2)
    f_stage(0)
    f_stage(1)
    z_stage(3)
    f_stage(2)
    f_stage(3)
    for p in range(PIECES):
        s_stage(p)
    for p in range(PIECES):
        for slot in range(4):
            across(p, slot % 2, slot // 2).wait()
        first(p).wait_send()
        second(p, 0).wait_send()
        second(p, 1).wait_send()

        def drain(owner, carry):
            @pl.when((owner <= z) & (z < depth - 1))
            def _():
                along_z(p, 0, owner).wait_send()

            @pl.when((owner >= z) & (z > 0))
            def _():
                along_z(p, 1, owner).wait_send()

            return carry

        lax.fori_loop(0, depth, drain, 0)


def gather(shards):
    dp, ctx = lax.axis_size("dp"), lax.axis_size("ctx")
    lead = (ctx // PAIR, PAIR, dp // PAIR, PAIR)
    dma = pltpu.SemaphoreType.DMA
    return pl.pallas_call(
        gather_kernel,
        out_shape=[jax.ShapeDtypeStruct(lead + shard.shape, shard.dtype) for shard in shards],
        in_specs=[pl.BlockSpec(memory_space=pl.ANY)] * PIECES,
        out_specs=[pl.BlockSpec(memory_space=pl.ANY)] * PIECES,
        scratch_shapes=[
            dma((PIECES,)),
            dma((2, PIECES, lead[2])),
            dma((2, PIECES, lead[2])),
            dma((PIECES,)),
            dma((PIECES,)),
            dma((PIECES, 2)),
            dma((PIECES, 2)),
            dma((PIECES, 4)),
            dma((PIECES, 4)),
        ],
        compiler_params=pltpu.CompilerParams(collective_id=0, has_side_effects=True),
        name="weight_gather",
    )(*shards)


def scatter_kernel(*refs):
    grads, sums = refs[:PIECES], refs[PIECES : 2 * PIECES]
    rest = refs[2 * PIECES :]
    locals_, cores, seconds, firsts, lines = (
        rest[i * PIECES : (i + 1) * PIECES] for i in range(5)
    )
    l_sem, z_send, z_recv, f_send, f_recv, s_send, s_recv, c_send, c_recv = rest[5 * PIECES :]
    depth = grads[0].shape[2]
    z, x, y, c = place()

    def sides(p):
        return (x, y) if p % 2 == 0 else (y, x)

    def block(p, f, s, core):
        return grads[p].at[s, core, :, f] if p % 2 == 0 else grads[p].at[f, core, :, s]

    def own(p, f_side, s_side):
        f, s = sides(p)
        f = f if f_side == 0 else 1 - f
        s = s if s_side == 0 else 1 - s
        slot = 2 * s_side + f_side
        return pltpu.make_async_copy(
            block(p, f, s, c), locals_[p].at[slot], l_sem.at[p, slot]
        )

    def across(p, f_side, s_side):
        f, s = sides(p)
        f = f if f_side == 0 else 1 - f
        s = s if s_side == 0 else 1 - s
        slot = 2 * s_side + f_side
        return remote(
            block(p, f, s, 1 - c),
            cores[p].at[slot],
            c_send.at[p, slot],
            c_recv.at[p, slot],
            device(z, x, y, 1 - c),
        )

    def second(p, f_side):
        where = device(z, x, 1 - y, c) if p % 2 == 0 else device(z, 1 - x, y, c)
        return remote(
            cores[p].at[2 + f_side],
            seconds[p].at[f_side],
            s_send.at[p, f_side],
            s_recv.at[p, f_side],
            where,
        )

    def first(p):
        where = device(z, 1 - x, y, c) if p % 2 == 0 else device(z, x, 1 - y, c)
        return remote(seconds[p].at[1], firsts[p], f_send.at[p], f_recv.at[p], where)

    def along_z(p, way, goal, source):
        return remote(
            source,
            lines[p].at[way, goal],
            z_send.at[way, p, goal],
            z_recv.at[way, p, goal],
            device(z + (1 if way == 0 else -1), x, y, c),
        )

    def add(target, source):
        def step(i, carry):
            total = target[i].astype(jnp.float32) + source[i].astype(jnp.float32)
            target[i] = total.astype(jnp.bfloat16)
            return carry

        lax.fori_loop(0, depth, step, 0)

    for p in range(PIECES):
        for slot in (3, 2, 1, 0):
            own(p, slot % 2, slot // 2).start()
    greet(z, x, y, c, depth)
    for p in range(PIECES):
        for slot in (3, 2, 1, 0):
            across(p, slot % 2, slot // 2).start()

    def core_sum(p, slot):
        own(p, slot % 2, slot // 2).wait()
        across(p, slot % 2, slot // 2).wait_recv()
        add(cores[p].at[slot], locals_[p].at[slot])

    def s_stage(p):
        for f_side in (1, 0):
            core_sum(p, 2 + f_side)
            second(p, f_side).start()

    def f_stage(p):
        for f_side in (1, 0):
            core_sum(p, f_side)
            second(p, f_side).wait_recv()
            add(seconds[p].at[f_side], cores[p].at[f_side])
            if f_side == 1:
                first(p).start()

    def pass_on(p, way, goal, has_before):
        @pl.when(has_before)
        def _():
            along_z(p, way, goal, lines[p].at[way, goal]).wait_recv()
            total = lines[p][way, goal].astype(jnp.float32) + firsts[p][goal].astype(jnp.float32)
            lines[p][way, goal] = total.astype(jnp.bfloat16)
            along_z(p, way, goal, lines[p].at[way, goal]).start()

        @pl.when(jnp.logical_not(has_before))
        def _():
            along_z(p, way, goal, firsts[p].at[goal]).start()

    def z_stage(p):
        first(p).wait_recv()
        add(firsts[p], seconds[p].at[0])

        def step(s, carry):
            @pl.when(z < depth - s)
            def _():
                pass_on(p, 0, depth - s, z > 0)

            @pl.when(z > s - 1)
            def _():
                pass_on(p, 1, s - 1, z < depth - 1)

            return carry

        lax.fori_loop(1, depth, step, 0)

    def finish(p):
        sums[p][...] = firsts[p][z].astype(jnp.float32)

        @pl.when(z > 0)
        def _():
            along_z(p, 0, z, lines[p].at[0, z]).wait_recv()
            sums[p][...] += lines[p][0, z].astype(jnp.float32)

        @pl.when(z < depth - 1)
        def _():
            along_z(p, 1, z, lines[p].at[1, z]).wait_recv()
            sums[p][...] += lines[p][1, z].astype(jnp.float32)

    for p in range(PIECES):
        s_stage(p)
    for p in range(PIECES):
        f_stage(p)
        if p > 0:
            z_stage(p - 1)
    z_stage(PIECES - 1)
    for p in range(PIECES):
        finish(p)
    for p in range(PIECES):
        for slot in range(4):
            across(p, slot % 2, slot // 2).wait_send()
        second(p, 0).wait_send()
        second(p, 1).wait_send()
        first(p).wait_send()

        def drain(goal, carry):
            @pl.when(goal > z)
            def _():
                along_z(p, 0, goal, firsts[p].at[goal]).wait_send()

            @pl.when(goal < z)
            def _():
                along_z(p, 1, goal, firsts[p].at[goal]).wait_send()

            return carry

        lax.fori_loop(0, depth, drain, 0)


def scatter(grads):
    depth = grads[0].shape[2]
    dma = pltpu.SemaphoreType.DMA
    shapes = [grad.shape[4:] for grad in grads]

    def slots(lead):
        return [pltpu.VMEM(lead + (depth,) + shape, jnp.bfloat16) for shape in shapes]

    return pl.pallas_call(
        scatter_kernel,
        out_shape=[jax.ShapeDtypeStruct(shape, jnp.float32) for shape in shapes],
        in_specs=[pl.BlockSpec(memory_space=pl.ANY)] * PIECES,
        out_specs=[pl.BlockSpec(memory_space=pltpu.VMEM)] * PIECES,
        scratch_shapes=slots((4,))
        + slots((4,))
        + slots((2,))
        + slots(())
        + slots((2,))
        + [
            dma((PIECES, 4)),
            dma((2, PIECES, depth)),
            dma((2, PIECES, depth)),
            dma((PIECES,)),
            dma((PIECES,)),
            dma((PIECES, 2)),
            dma((PIECES, 2)),
            dma((PIECES, 4)),
            dma((PIECES, 4)),
        ],
        compiler_params=pltpu.CompilerParams(
            collective_id=1, has_side_effects=True, vmem_limit_bytes=58 * 1024 * 1024
        ),
        name="grad_scatter",
    )(*grads)


EXTRA = 8


def fetch(gain_attn, w_query, w_key, w_value, w_out, gain_ffn, w_gate, w_up, w_down):
    rows = w_query.shape[0]
    mixed = jnp.concatenate([w_query, w_key, w_value, w_out], axis=1)
    gains = jnp.pad(
        jnp.stack([gain_attn, gain_ffn]), ((0, EXTRA - 2), (0, mixed.shape[1] - rows))
    )
    full_mixed, full_gate, full_up, full_down = gather(
        [jnp.concatenate([mixed, gains], axis=0), w_gate, w_up, w_down]
    )
    dp, ctx = lax.axis_size("dp"), lax.axis_size("ctx")

    def stacked(array):
        return array.reshape(ctx, dp * array.shape[4], array.shape[5])

    def beside(array):
        return jnp.concatenate([array[block] for block in range(ctx)], axis=1)

    corner = full_mixed.reshape((ctx, dp) + full_mixed.shape[4:])[0]
    one = corner[:, rows, :rows].reshape(-1)
    two = corner[:, rows + 1, :rows].reshape(-1)
    blocks = stacked(full_mixed[:, :, :, :, :rows])
    parts = []
    low = 0
    for weight in (w_query, w_key, w_value, w_out):
        high = low + weight.shape[1]
        parts.append(beside(blocks[:, :, low:high]))
        low = high
    return (*parts, beside(stacked(full_gate)), beside(stacked(full_up)), beside(stacked(full_down)), one, two)


def settle(grad_one, grad_two, mixed_pairs, gate_pair, up_pair, down_pair):
    dp, ctx = lax.axis_size("dp"), lax.axis_size("ctx")
    lead = (ctx // PAIR, PAIR, dp // PAIR, PAIR)

    def blocks(pairs):
        made = []
        for block in range(ctx):
            columns = []
            for former, latters in pairs:
                cuts = []
                for latter in latters:
                    wide = latter.shape[1] // ctx
                    cuts.append(latter[:, block * wide : (block + 1) * wide])
                latter = cuts[0] if len(cuts) == 1 else jnp.concatenate(cuts, axis=1)
                columns.append(outer_sum(former, latter).astype(jnp.bfloat16))
            made.append(columns[0] if len(columns) == 1 else jnp.concatenate(columns, axis=1))
        height, wide = made[0].shape
        return jnp.stack(made).reshape(ctx, dp, height // dp, wide)

    mixed = blocks(mixed_pairs)
    rows, wide = mixed.shape[2:]
    gains = jnp.stack([grad_one.reshape(dp, rows), grad_two.reshape(dp, rows)], axis=1)
    gains = jnp.pad(gains.astype(jnp.bfloat16), ((0, 0), (0, EXTRA - 2), (0, wide - rows)))
    gains = jnp.broadcast_to(gains[None], (ctx,) + gains.shape)
    mixed = jnp.concatenate([mixed, gains], axis=2)
    pieces = [mixed, blocks([gate_pair]), blocks([up_pair]), blocks([down_pair])]
    own_mixed, own_gate, own_up, own_down = scatter(
        [piece.reshape(lead + piece.shape[2:]) for piece in pieces]
    )
    cuts = []
    low = 0
    for latter in (*mixed_pairs[0][1], *mixed_pairs[1][1]):
        high = low + latter.shape[1] // ctx
        cuts.append(own_mixed[:rows, low:high])
        low = high
    return (
        own_mixed[rows, :rows],
        *cuts,
        own_mixed[rows + 1, :rows],
        own_gate,
        own_up,
        own_down,
    )


def masked_scores(queries, key_block, allowed, factor):
    scores = (
        jnp.einsum("mcgd,mld->mgcl", queries, key_block, preferred_element_type=jnp.float32)
        * factor
    )
    return jnp.where(allowed, scores, -1e30)


def attend(operands, allowed, factor):
    queries, key_block, value_block = operands
    scores = masked_scores(queries, key_block, allowed, factor)
    peak = jnp.max(scores, axis=-1, keepdims=True)
    raised = jnp.exp(scores - peak)
    summed = jnp.sum(raised, axis=-1, keepdims=True)
    shares = (raised / summed).astype(jnp.bfloat16)
    blended = jnp.einsum("mgcl,mld->mcgd", shares, value_block, preferred_element_type=jnp.float32)
    return (blended.astype(jnp.bfloat16), peak + jnp.log(summed))


def attend_back(operands, allowed, factor):
    queries, key_block, value_block, upstream, logsum = operands
    scores = masked_scores(queries, key_block, allowed, factor)
    shares = jnp.exp(scores - logsum)
    d_values = jnp.einsum(
        "mgcl,mcgd->mld", shares.astype(jnp.bfloat16), upstream, preferred_element_type=jnp.float32
    )
    d_shares = jnp.einsum(
        "mcgd,mld->mgcl", upstream, value_block, preferred_element_type=jnp.float32
    )
    row_dot = jnp.sum(d_shares * shares, axis=-1, keepdims=True)
    d_scores = (shares * (d_shares - row_dot)).astype(jnp.bfloat16)
    d_queries = (
        jnp.einsum("mgcl,mld->mcgd", d_scores, key_block, preferred_element_type=jnp.float32)
        * factor
    )
    d_keys = (
        jnp.einsum("mgcl,mcgd->mld", d_scores, queries, preferred_element_type=jnp.float32) * factor
    )
    return (d_queries, d_keys, d_values)


def on_device(
    tokens,
    lengths,
    gain_attn,
    w_query,
    w_key,
    w_value,
    w_out,
    gain_ffn,
    w_gate,
    w_up,
    w_down,
    grad_out,
):
    seq_count, span_len, width = tokens.shape
    groups = lax.axis_size("ctx")
    length = span_len * groups
    ctx_rank = lax.axis_index("ctx")
    batch_size = seq_count
    per_kv = HEADS // KV_HEADS
    query_width = HEADS * HEAD_DIM
    key_width = KV_HEADS * HEAD_DIM
    factor = HEAD_DIM ** (-0.5)
    half_dim = HEAD_DIM // 2
    inverse = THETA ** (-(jnp.arange(half_dim, dtype=jnp.float32) * 2.0 / HEAD_DIM))
    query_pos = ctx_rank * span_len + jnp.arange(span_len, dtype=jnp.int32)
    angles = query_pos.astype(jnp.float32)[:, None] * inverse[None, :]
    cosine = jnp.cos(angles)
    sine_part = jnp.sin(angles)
    cos_query = cosine[:, None, None, :]
    sin_query = sine_part[:, None, None, :]
    cos_key = cosine[:, None, :]
    sin_key = sine_part[:, None, :]
    key_pos = jnp.arange(length, dtype=jnp.int32)
    causal = key_pos[None, :] <= query_pos[:, None]
    rows = batch_size * span_len
    shards = (gain_attn, w_query, w_key, w_value, w_out, gain_ffn, w_gate, w_up, w_down)
    forward_weights = fetch(*shards)
    (
        full_query,
        full_key,
        full_value,
        full_out,
        full_gate,
        full_up,
        full_down,
        full_one,
        full_two,
    ) = forward_weights
    gain_one = full_one.astype(jnp.float32)
    gain_two = full_two.astype(jnp.float32)
    inputs = tokens.astype(jnp.float32).reshape(rows, width)
    valid_len = lengths
    allowed = causal[None, None] & (
        key_pos[None, None, None, :] < valid_len[:, None, None, None]
    )
    normed_attn = rms_scale(inputs, gain_one).astype(jnp.bfloat16)
    queries = product(normed_attn, full_query).reshape(
        batch_size, span_len, KV_HEADS, per_kv, HEAD_DIM
    )
    queries = rotate(queries, cos_query, sin_query).astype(jnp.bfloat16)
    key_own = product(normed_attn, full_key).reshape(batch_size, span_len, KV_HEADS, HEAD_DIM)
    key_own = (
        rotate(key_own, cos_key, sin_key)
        .astype(jnp.bfloat16)
        .reshape(batch_size, span_len, key_width)
    )
    value_own = (
        product(normed_attn, full_value)
        .astype(jnp.bfloat16)
        .reshape(batch_size, span_len, key_width)
    )
    key_all, value_all = (
        lax.all_gather(key_own, "ctx", axis=1, tiled=True),
        lax.all_gather(value_own, "ctx", axis=1, tiled=True),
    )
    head_query = jnp.moveaxis(queries, 2, 0)
    head_key = jnp.moveaxis(key_all.reshape(batch_size, length, KV_HEADS, HEAD_DIM), 2, 0)
    head_value = jnp.moveaxis(value_all.reshape(batch_size, length, KV_HEADS, HEAD_DIM), 2, 0)
    blended, logsum = lax.map(
        partial(attend, allowed=allowed, factor=factor), (head_query, head_key, head_value)
    )
    attended = jnp.moveaxis(blended, 0, 2).reshape(rows, query_width)
    hidden = inputs + product(attended, full_out)
    normed_ffn = rms_scale(hidden, gain_two).astype(jnp.bfloat16)
    gating = product(normed_ffn, full_gate)
    up_proj = product(normed_ffn, full_up)
    inner = silu_gate(gating, up_proj).astype(jnp.bfloat16)
    result = hidden + product(inner, full_down)
    output_all = result.astype(jnp.bfloat16).reshape(batch_size, span_len, width)
    upstream = grad_out.astype(jnp.float32).reshape(rows, width)
    d_down = upstream.astype(jnp.bfloat16)
    d_inner = against(d_down, full_down)
    gate_pull = jax.vjp(silu_gate, gating, up_proj)[1]
    d_gating, d_up = gate_pull(d_inner)
    d_gating = d_gating.astype(jnp.bfloat16)
    d_up = d_up.astype(jnp.bfloat16)
    d_normed_ffn = against(d_gating, full_gate) + against(d_up, full_up)
    ffn_pull = jax.vjp(rms_scale, hidden, full_two.astype(jnp.float32))[1]
    d_hidden_part, grad_two = ffn_pull(d_normed_ffn)
    d_hidden = upstream + d_hidden_part
    d_attn = d_hidden.astype(jnp.bfloat16)
    d_attended = against(d_attn, full_out).astype(jnp.bfloat16)
    head_upstream = jnp.moveaxis(
        d_attended.reshape(batch_size, span_len, KV_HEADS, per_kv, HEAD_DIM), 2, 0
    )
    d_query_h, d_key_h, d_value_h = lax.map(
        partial(attend_back, allowed=allowed, factor=factor),
        (head_query, head_key, head_value, head_upstream, logsum),
    )
    d_key_full = jnp.moveaxis(d_key_h, 0, 2).reshape(batch_size, length, key_width)
    d_value_full = jnp.moveaxis(d_value_h, 0, 2).reshape(batch_size, length, key_width)
    d_key_own, d_value_own = (
        lax.psum_scatter(d_key_full, "ctx", scatter_dimension=1, tiled=True),
        lax.psum_scatter(d_value_full, "ctx", scatter_dimension=1, tiled=True),
    )
    d_query = (
        rotate(jnp.moveaxis(d_query_h, 0, 2), cos_query, -sin_query)
        .astype(jnp.bfloat16)
        .reshape(rows, query_width)
    )
    d_key = (
        rotate(d_key_own.reshape(batch_size, span_len, KV_HEADS, HEAD_DIM), cos_key, -sin_key)
        .astype(jnp.bfloat16)
        .reshape(rows, key_width)
    )
    d_value = d_value_own.astype(jnp.bfloat16).reshape(rows, key_width)
    d_normed_attn = (
        against(d_query, full_query) + against(d_key, full_key) + against(d_value, full_value)
    )
    attn_pull = jax.vjp(rms_scale, inputs, full_one.astype(jnp.float32))[1]
    d_input_part, grad_one = attn_pull(d_normed_attn)
    grads_all = (d_hidden + d_input_part).astype(jnp.bfloat16).reshape(batch_size, span_len, width)
    owned = settle(
        grad_one,
        grad_two,
        [(normed_attn, (d_query, d_key, d_value)), (attended, (d_attn,))],
        (normed_ffn, (d_gating,)),
        (normed_ffn, (d_up,)),
        (inner, (d_down,)),
    )
    return (
        output_all,
        grads_all,
        owned[0],
        owned[1],
        owned[2],
        owned[3],
        owned[4],
        owned[5],
        owned[6],
        owned[7],
        owned[8],
    )


def solution(mesh):
    return jax.shard_map(
        on_device,
        mesh=mesh,
        in_specs=(
            P("dp", "ctx", None),
            P("dp"),
            P("dp"),
            P("dp", "ctx"),
            P("dp", "ctx"),
            P("dp", "ctx"),
            P("dp", "ctx"),
            P("dp"),
            P("dp", "ctx"),
            P("dp", "ctx"),
            P("dp", "ctx"),
            P("dp", "ctx", None),
        ),
        out_specs=(
            P("dp", "ctx", None),
            P("dp", "ctx", None),
            P("dp"),
            P("dp", "ctx"),
            P("dp", "ctx"),
            P("dp", "ctx"),
            P("dp", "ctx"),
            P("dp"),
            P("dp", "ctx"),
            P("dp", "ctx"),
            P("dp", "ctx"),
        ),
        check_vma=False,
    )
```
